32 devices in a mesh: orb: 4 (over x, core), dom: 8 (over z, y).
Axes of the slice: x: 2, y: 2, z: 4, core: 2. Of those that a mesh axis runs over, the one named last changes fastest.
Arguments:
- orbitals: float32 [768, 32, 8, 128], P('orb', 'dom'), may hold values from -6 to 6
- potential: float32 [32, 8, 128], P('dom'), may hold values from -1 to 3
- prev_gradient: float32 [768, 32, 8, 128], P('orb', 'dom'), may hold values from -24 to 24
- prev_direction: float32 [768, 32, 8, 128], P('orb', 'dom'), may hold values from -24 to 24
Outputs:
- new_orbitals: float32 [768, 32, 8, 128], P('orb', 'dom')
- new_direction: float32 [768, 32, 8, 128], P('orb', 'dom')
- gradient: float32 [768, 32, 8, 128], P('orb', 'dom')
The draws below stay inside these ranges and needn't reach their ends.
All inputs are finite; a program needn't handle non-finite values.
Results may differ from the reference program's by a relative error of at most 0.0002.
Values sent between devices are 32-bit elements; how exact they have to be, the bound alone decides.
A program may use at most 128 MiB of HBM per device.

```python
import jax
import jax.numpy as jnp
from jax import lax

NORB = 768
NX = 128
NY = 8
NZ = 32


def block_levels(rng, extent, shards, smallest, largest):
    factor_of = 1.0
    for position, shards_of in shards:
        heights = jax.random.uniform(jax.random.fold_in(jax.random.fold_in(rng, 6), position), (shards_of,), jnp.float32, smallest / len(shards), largest / len(shards))
        factor_of = factor_of * jnp.repeat(jnp.exp(heights), extent[position] // shards_of).reshape((-1,) + (1,) * (len(extent) - 1 - position))
    return factor_of


def scatter_about(stream_key, dims, scale, reach, cuts=(), dtype=jnp.bfloat16):
    values = scale * jax.random.normal(stream_key, dims, jnp.float32)
    if cuts:
        values = values * block_levels(stream_key, dims, cuts, -0.22, 0.18)
    return jnp.clip(values, -reach, reach).astype(dtype)


def setup_inputs(seed: int = 0) -> dict:
    key_of = jax.random.split(jax.random.key(seed), 5)
    return {
        "orbitals": scatter_about(key_of[0], (NORB, NZ, NY, NX), 1.0, 6.0, ((0, 4), (1, 8)), jnp.float32),
        "potential": jnp.clip(-1.0 + 4.0 * jax.random.uniform(key_of[1], (NZ, NY, NX), jnp.float32) ** block_levels(key_of[1], (NZ, NY, NX), ((0, 8),), -0.2, 0.2), -1.0, 3.0),
        "prev_gradient": scatter_about(key_of[2], (NORB, NZ, NY, NX), 4.0, 24.0, ((0, 4), (1, 8)), jnp.float32),
        "prev_direction": scatter_about(key_of[3], (NORB, NZ, NY, NX), 4.0, 24.0, ((0, 4), (1, 8)), jnp.float32),
    }


coeffs = (-205.0 / 72.0, 8.0 / 5.0, -1.0 / 5.0, 8.0 / 315.0, -1.0 / 560.0)
step_length = 0.05


def laplace(padded, planes, lines, columns):
    center = padded[:, 4:4 + planes, 4:4 + lines, 4:4 + columns]
    total = 3.0 * coeffs[0] * center
    for offset in range(1, 5):
        total = total + coeffs[offset] * (padded[:, 4 + offset:4 + offset + planes, 4:4 + lines, 4:4 + columns] + padded[:, 4 - offset:4 - offset + planes, 4:4 + lines, 4:4 + columns])
        total = total + coeffs[offset] * (padded[:, 4:4 + planes, 4 + offset:4 + offset + lines, 4:4 + columns] + padded[:, 4:4 + planes, 4 - offset:4 - offset + lines, 4:4 + columns])
        total = total + coeffs[offset] * (padded[:, 4:4 + planes, 4:4 + lines, 4 + offset:4 + offset + columns] + padded[:, 4:4 + planes, 4:4 + lines, 4 - offset:4 - offset + columns])
    return total


def highdot(left, right):
    return jnp.dot(left, right, precision=lax.Precision.HIGHEST, preferred_element_type=jnp.float32)


def reference(orbitals, potential, prev_gradient, prev_direction):
    count = orbitals.shape[0]
    padded = jnp.pad(orbitals, ((0, 0), (4, 4), (4, 4), (4, 4)))
    lap = laplace(padded, orbitals.shape[1], orbitals.shape[2], orbitals.shape[3])
    image = -0.5 * lap + potential[None] * orbitals
    cmat = orbitals.reshape(count, -1)
    hmat_rows = image.reshape(count, -1)
    cells = cmat.shape[1]
    correlation = highdot(cmat, cmat.T) / cells
    hamilton = highdot(cmat, hmat_rows.T) / cells
    grad = 4.0 * hmat_rows - 2.0 * highdot(correlation.T, hmat_rows) - 2.0 * highdot(hamilton.T, cmat)
    grad = grad.reshape(orbitals.shape)
    both = jnp.sum(grad * grad)
    cross = jnp.sum(grad * prev_gradient)
    before = jnp.sum(prev_gradient * prev_gradient)
    beta = (both - cross) / before
    direction = -grad + beta * prev_direction
    return orbitals + step_length * direction, direction, grad
```

```python
import functools

import jax
import jax.numpy as jnp
from jax import lax
from jax.experimental import pallas as pl
from jax.experimental.pallas import tpu as pltpu
from jax.sharding import PartitionSpec as P

coeffs = (-205.0 / 72.0, 8.0 / 5.0, -1.0 / 5.0, 8.0 / 315.0, -1.0 / 560.0)
step_length = 0.05
width = 4
MESH = pl.DeviceIdType.MESH
NT = (((1,), (1,)), ((), ()))
NN = (((1,), (0,)), ((), ()))


def split(value):
    high = value.astype(jnp.bfloat16)
    return high, (value - high.astype(jnp.float32)).astype(jnp.bfloat16)


def dot3(left, right, dims):
    def dot(a, b):
        return lax.dot_general(a, b, dims, preferred_element_type=jnp.float32)

    return dot(left[0], right[0]) + (dot(left[0], right[1]) + dot(left[1], right[0]))


def kernel(
    cfg, c_hbm, pot, pg_hbm, grad_out, stat_out,
    orbs, images, halo, pg, part, inbox, full, acc, near, far,
    local_sem, halo_s, halo_r, c_s, c_r, cf_s, cf_r, i_s, i_r, if_s, if_r,
    rs_s, rs_r, ag_s, ag_r, n_s, n_r, f_s, f_r,
):
    no, nd, planes, lines, block, chunks = cfg
    rows = planes * lines
    edge = width * lines
    size = block // chunks
    nx = no // 2
    count = no * block
    share = block // nd
    cells = rows * 128 * nd
    o, d = lax.axis_index("orb"), lax.axis_index("dom")
    core = lax.rem(o, 2)
    column = o // 2
    mate = column * 2 + (1 - core)
    tos = [lax.rem(column + j, nx) * 2 + core for j in range(1, nx)]
    froms = [lax.rem(column - j + nx, nx) * 2 + core for j in range(1, nx)]

    load = pltpu.make_async_copy(c_hbm, orbs.at[o], local_sem.at[0])
    load.start()
    for r in range(rows):
        pltpu.make_async_copy(
            pg_hbm.at[:, r // lines, r % lines, :], pg.at[r], local_sem.at[1]
        ).start()

    barrier = pltpu.get_barrier_semaphore()
    for j in range(1, no):
        pl.semaphore_signal(barrier, inc=1, device_id=(lax.rem(o + j, no), d), device_id_type=MESH)
    for j in range(1, nd):
        pl.semaphore_signal(barrier, inc=1, device_id=(o, lax.rem(d + j, nd)), device_id_type=MESH)
    load.wait()
    pl.semaphore_wait(barrier, no + nd - 2)

    def cut(c):
        return pl.ds(pl.multiple_of(c * size, 8), size)

    def remote(src, dst, send, recv, device):
        return pltpu.make_async_remote_copy(
            src_ref=src, dst_ref=dst, send_sem=send, recv_sem=recv, device_id=device, device_id_type=MESH
        )

    def up(c):
        return remote(
            orbs.at[o, pl.ds(rows - edge, edge), cut(c), :], halo.at[0, :, cut(c), :],
            halo_s.at[0, c], halo_r.at[0, c], (o, lax.rem(d + 1, nd)),
        )

    def down(c):
        return remote(
            orbs.at[o, pl.ds(0, edge), cut(c), :], halo.at[1, :, cut(c), :],
            halo_s.at[1, c], halo_r.at[1, c], (o, lax.rem(d + nd - 1, nd)),
        )

    def start_halo(c):
        @pl.when(d < nd - 1)
        def _():
            up(c).start()

        @pl.when(d > 0)
        def _():
            down(c).start()

    def spread(buf, send, recv, c, j):
        to = mate if j == 0 else tos[j - 1]
        ref = buf.at[o, :, cut(c), :]
        return remote(ref, ref, send.at[j, c], recv.at[j, c], (to, d))

    def forward(buf, send, recv, c, j):
        ref = buf.at[froms[j - 1], :, cut(c), :]
        return remote(ref, ref, send.at[j - 1, c], recv.at[j - 1, c], (mate, d))

    def start_spread(buf, send, recv, c):
        for j in list(range(1, nx)) + [0]:
            spread(buf, send, recv, c, j).start()

    def pass_on(buf, recv, send_f, recv_f, c):
        for j in range(1, nx):
            spread(buf, recv, recv, c, j).wait_recv()
            forward(buf, send_f, recv_f, c, j).start()

    start_halo(0)
    if chunks > 1:
        start_halo(1)
    for c in range(chunks):
        start_spread(orbs, c_s, c_r, c)

    @pl.when(d == 0)
    def _():
        halo[0] = jnp.zeros(halo.shape[1:], jnp.float32)

    @pl.when(d == nd - 1)
    def _():
        halo[1] = jnp.zeros(halo.shape[1:], jnp.float32)

    away = jnp.abs(
        lax.broadcasted_iota(jnp.int32, (128, 128), 0) - lax.broadcasted_iota(jnp.int32, (128, 128), 1)
    )
    band = jnp.zeros((128, 128), jnp.float32)
    for k in range(1, width + 1):
        band = jnp.where(away == k, -0.5 * coeffs[k], band)
    band = split(band)

    def stencil(c):
        at = cut(c)

        def line(p, y):
            if p < 0:
                return halo[0, (p + width) * lines + y, at, :]
            if p >= planes:
                return halo[1, (p - planes) * lines + y, at, :]
            return orbs[o, p * lines + y, at, :]

        for p in range(planes):
            mid = orbs[o, pl.ds(p * lines, lines), at, :]
            along = dot3(split(mid.reshape(lines * size, 128)), band, NN).reshape(lines, size, 128)
            for y in range(lines):
                total = along[y] + (pot[p * lines + y] - 1.5 * coeffs[0]) * line(p, y)
                for k in range(1, width + 1):
                    near_ = line(p + k, y) + line(p - k, y)
                    if y + k < lines:
                        near_ = near_ + line(p, y + k)
                    if y - k >= 0:
                        near_ = near_ + line(p, y - k)
                    total = total + (-0.5 * coeffs[k]) * near_
                images[o, p * lines + y, at, :] = total

    def step(c):
        @pl.when(d > 0)
        def _():
            up(c).wait_recv()

        @pl.when(d < nd - 1)
        def _():
            down(c).wait_recv()

        stencil(c)
        start_spread(images, i_s, i_r, c)
        pass_on(orbs, c_r, cf_s, cf_r, c)

    group = next(g for g in (4, 2, 1) if rows % g == 0)

    def gathered(buf, r):
        return jnp.concatenate(
            [jnp.concatenate([buf[s, r * group + i] for i in range(group)], axis=1) for s in range(no)], axis=0
        )

    def mine(buf, r):
        return jnp.concatenate([buf[o, r * group + i] for i in range(group)], axis=1)

    def overlaps(buf, slot):
        acc[...] = jnp.zeros(acc.shape, jnp.float32)

        def body(r, carry):
            acc[...] += dot3(split(mine(buf, r)), split(gathered(orbs, r)), NT)
            return carry

        lax.fori_loop(0, rows // group, body, 0)
        for e in range(nd):
            part[slot, e] = acc[e * share : (e + 1) * share, :]

    def scatter(slot, j):
        e = lax.rem(d + j, nd)
        return remote(
            part.at[slot, e], inbox.at[slot, d], rs_s.at[slot, j - 1], rs_r.at[slot, j - 1], (o, e)
        )

    def share_out(slot, j):
        e = lax.rem(d + j, nd)
        ref = full.at[slot, d]
        return remote(ref, ref, ag_s.at[slot, j - 1], ag_r.at[slot, j - 1], (o, e))

    def reduce_start(slot):
        for j in range(1, nd):
            scatter(slot, j).start()
        inbox[slot, d] = part[slot, d]

    def reduce_mid(slot):
        for j in range(1, nd):
            scatter(slot, j).wait_recv()
        total = inbox[slot, 0]
        for e in range(1, nd):
            total = total + inbox[slot, e]
        full[slot, d] = total * (1.0 / cells)
        for j in range(1, nd):
            share_out(slot, j).start()

    def reduce_end(slot):
        for j in range(1, nd):
            share_out(slot, j).wait_recv()

    def early(c, carry):
        @pl.when(c + 2 < chunks)
        def _():
            start_halo(c + 2)

        step(c)

        @pl.when(c > 0)
        def _():
            pass_on(images, i_r, if_s, if_r, c - 1)

        return carry

    lax.fori_loop(0, chunks - 1, early, 0)
    last = chunks - 1
    pass_on(orbs, c_r, cf_s, cf_r, last)

    def arrive(c, carry):
        spread(orbs, c_s, c_r, c, 0).wait_recv()
        for j in range(1, nx):
            forward(orbs, cf_s, cf_r, c, j).wait_recv()
        return carry

    lax.fori_loop(0, chunks, arrive, 0)
    overlaps(orbs, 0)
    reduce_start(0)

    @pl.when(d > 0)
    def _():
        up(last).wait_recv()

    @pl.when(d < nd - 1)
    def _():
        down(last).wait_recv()

    stencil(last)
    start_spread(images, i_s, i_r, last)
    if chunks > 1:
        pass_on(images, i_r, if_s, if_r, last - 1)
    reduce_mid(0)
    overlaps(images, 1)
    reduce_start(1)
    pass_on(images, i_r, if_s, if_r, last)
    reduce_end(0)
    reduce_mid(1)

    def arrive_images(c, carry):
        spread(images, i_s, i_r, c, 0).wait_recv()
        for j in range(1, nx):
            forward(images, if_s, if_r, c, j).wait_recv()
        return carry

    lax.fori_loop(0, chunks, arrive_images, 0)
    reduce_end(1)
    pltpu.make_async_copy(pg, pg, local_sem.at[1]).wait()

    def matrix(slot):
        return jnp.concatenate([full[slot, e] for e in range(nd)], axis=0)

    def fold(value):
        return jnp.sum(value.reshape(block // 8, 8, 128), axis=0)

    correlation, hamilton = split(matrix(0)), split(matrix(1))

    def gradient(r, sums):
        mixed = dot3(correlation, split(gathered(images, r)), NN) + dot3(hamilton, split(gathered(orbs, r)), NN)
        both, cross, before = sums
        for i in range(group):
            at = r * group + i
            grad = 4.0 * images[o, at] - 2.0 * mixed[:, i * 128 : (i + 1) * 128]
            grad_out[at] = grad
            old = pg[at]
            both = both + fold(grad * grad)
            cross = cross + fold(grad * old)
            before = before + fold(old * old)
        return both, cross, before

    zero = jnp.zeros((8, 128), jnp.float32)
    sums = lax.fori_loop(0, rows // group, gradient, (zero, zero, zero))

    near[o] = jnp.concatenate(
        [jnp.sum(s, axis=0, keepdims=True) for s in sums] + [jnp.zeros((5, 128), jnp.float32)], axis=0
    )

    def tell(buf, at, j, send, recv, device):
        return remote(buf.at[at], buf.at[at], send.at[j - 1], recv.at[j - 1], device)

    def near_copy(j):
        return tell(near, o, j, n_s, n_r, (lax.rem(o + j, no), d))

    def far_copy(j):
        return tell(far, d, j, f_s, f_r, (o, lax.rem(d + j, nd)))

    for j in range(1, no):
        near_copy(j).start()
    for j in range(1, no):
        near_copy(j).wait_recv()
    total = near[0]
    for s in range(1, no):
        total = total + near[s]
    far[d] = total
    for j in range(1, nd):
        far_copy(j).start()
    for j in range(1, nd):
        far_copy(j).wait_recv()
    total = far[0]
    for s in range(1, nd):
        total = total + far[s]
    stat_out[...] = total

    def drain(c, carry):
        @pl.when(d < nd - 1)
        def _():
            up(c).wait_send()

        @pl.when(d > 0)
        def _():
            down(c).wait_send()

        for j in range(nx):
            spread(orbs, c_s, c_r, c, j).wait_send()
            spread(images, i_s, i_r, c, j).wait_send()
        for j in range(1, nx):
            forward(orbs, cf_s, cf_r, c, j).wait_send()
            forward(images, if_s, if_r, c, j).wait_send()
        return carry

    lax.fori_loop(0, chunks, drain, 0)
    for j in range(1, nd):
        for slot in range(2):
            scatter(slot, j).wait_send()
            share_out(slot, j).wait_send()
        far_copy(j).wait_send()
    for j in range(1, no):
        near_copy(j).wait_send()


def on_device(no, nd, orbitals, potential, prev_gradient, prev_direction):
    block, planes, lines, columns = orbitals.shape
    rows = planes * lines
    chunks = next(n for n in (6, 4, 3, 2, 1) if block % (8 * n) == 0)
    nx = no // 2
    share = block // nd
    f32 = jnp.float32
    dma = pltpu.SemaphoreType.DMA
    turned = orbitals.reshape(block, rows, columns).transpose(1, 0, 2)
    links = max(nx - 1, 1)
    grad, stats = pl.pallas_call(
        functools.partial(kernel, (no, nd, planes, lines, block, chunks)),
        out_shape=(
            jax.ShapeDtypeStruct((rows, block, columns), f32),
            jax.ShapeDtypeStruct((8, columns), f32),
        ),
        in_specs=[
            pl.BlockSpec(memory_space=pl.ANY),
            pl.BlockSpec(memory_space=pltpu.VMEM),
            pl.BlockSpec(memory_space=pl.ANY),
        ],
        out_specs=(pl.BlockSpec(memory_space=pltpu.VMEM), pl.BlockSpec(memory_space=pltpu.VMEM)),
        scratch_shapes=[
            pltpu.VMEM((no, rows, block, columns), f32),
            pltpu.VMEM((no, rows, block, columns), f32),
            pltpu.VMEM((2, width * lines, block, columns), f32),
            pltpu.VMEM((rows, block, columns), f32),
            pltpu.VMEM((2, nd, share, no * block), f32),
            pltpu.VMEM((2, nd, share, no * block), f32),
            pltpu.VMEM((2, nd, share, no * block), f32),
            pltpu.VMEM((block, no * block), f32),
            pltpu.VMEM((no, 8, columns), f32),
            pltpu.VMEM((nd, 8, columns), f32),
            dma((2,)),
            dma((2, chunks)), dma((2, chunks)),
            dma((nx, chunks)), dma((nx, chunks)), dma((links, chunks)), dma((links, chunks)),
            dma((nx, chunks)), dma((nx, chunks)), dma((links, chunks)), dma((links, chunks)),
            dma((2, nd - 1)), dma((2, nd - 1)), dma((2, nd - 1)), dma((2, nd - 1)),
            dma((no - 1,)), dma((no - 1,)), dma((nd - 1,)), dma((nd - 1,)),
        ],
        compiler_params=pltpu.CompilerParams(
            collective_id=0, has_side_effects=True, vmem_limit_bytes=60 * 1024 * 1024
        ),
    )(turned, potential.reshape(rows, 1, columns), prev_gradient)
    grad = grad.transpose(1, 0, 2).reshape(orbitals.shape)
    both, cross, before = jnp.sum(stats[0]), jnp.sum(stats[1]), jnp.sum(stats[2])
    beta = (both - cross) / before
    direction = -grad + beta * prev_direction
    return (orbitals + step_length * direction, direction, grad)


def solution(mesh):
    spec = P("orb", "dom", None, None)
    return jax.shard_map(
        functools.partial(on_device, mesh.shape["orb"], mesh.shape["dom"]),
        mesh=mesh,
        in_specs=(spec, P("dom", None, None), spec, spec),
        out_specs=(spec, spec, spec),
        check_vma=False,
    )
```

```python
import functools

import jax
import jax.numpy as jnp
from jax import lax
from jax.experimental import pallas as pl
from jax.experimental.pallas import tpu as pltpu
from jax.sharding import PartitionSpec as P

coeffs = (-205.0 / 72.0, 8.0 / 5.0, -1.0 / 5.0, 8.0 / 315.0, -1.0 / 560.0)
step_length = 0.05
width = 4
MESH = pl.DeviceIdType.MESH
NT = (((1,), (1,)), ((), ()))
NN = (((1,), (0,)), ((), ()))


def split(value):
    high = value.astype(jnp.bfloat16)
    return high, (value - high.astype(jnp.float32)).astype(jnp.bfloat16)


def dot3(left, right, dims):
    def dot(a, b):
        return lax.dot_general(a, b, dims, preferred_element_type=jnp.float32)

    return dot(left[0], right[0]) + (dot(left[0], right[1]) + dot(left[1], right[0]))


def kernel(
    cfg, c_hbm, pot, pg_hbm, grad_out, stat_out,
    orbs, images, halo, pg, part0, inbox0, full0, part1, inbox1, full1, acc, near, far,
    local_sem, halo_s, halo_r, c_s, c_r, cf_s, cf_r, i_s, i_r, if_s, if_r,
    rs_s, rs_r, ag_s, ag_r, n_s, n_r, f_s, f_r,
):
    no, nd, planes, lines, block, chunks = cfg
    rows = planes * lines
    edge = width * lines
    size = block // chunks
    nx = no // 2
    count = no * block
    cells = rows * 128 * nd
    last = chunks - 1
    heights = (block + last * size, size)
    part, inbox, full = (part0, part1), (inbox0, inbox1), (full0, full1)
    o, d = lax.axis_index("orb"), lax.axis_index("dom")
    core = lax.rem(o, 2)
    column = o // 2
    mate = column * 2 + (1 - core)
    tos = [lax.rem(column + j, nx) * 2 + core for j in range(1, nx)]
    froms = [lax.rem(column - j + nx, nx) * 2 + core for j in range(1, nx)]

    load = pltpu.make_async_copy(c_hbm, orbs.at[o], local_sem.at[0])
    load.start()
    for r in range(rows):
        pltpu.make_async_copy(
            pg_hbm.at[:, r // lines, r % lines, :], pg.at[r], local_sem.at[1]
        ).start()

    barrier = pltpu.get_barrier_semaphore()
    for j in range(1, no):
        pl.semaphore_signal(barrier, inc=1, device_id=(lax.rem(o + j, no), d), device_id_type=MESH)
    for j in range(1, nd):
        pl.semaphore_signal(barrier, inc=1, device_id=(o, lax.rem(d + j, nd)), device_id_type=MESH)
    load.wait()
    pl.semaphore_wait(barrier, no + nd - 2)

    def cut(c):
        return pl.ds(pl.multiple_of(c * size, 8), size)

    def remote(src, dst, send, recv, device):
        return pltpu.make_async_remote_copy(
            src_ref=src, dst_ref=dst, send_sem=send, recv_sem=recv, device_id=device, device_id_type=MESH
        )

    def up(c):
        return remote(
            orbs.at[o, pl.ds(rows - edge, edge), cut(c), :], halo.at[0, :, cut(c), :],
            halo_s.at[0, c], halo_r.at[0, c], (o, lax.rem(d + 1, nd)),
        )

    def down(c):
        return remote(
            orbs.at[o, pl.ds(0, edge), cut(c), :], halo.at[1, :, cut(c), :],
            halo_s.at[1, c], halo_r.at[1, c], (o, lax.rem(d + nd - 1, nd)),
        )

    def start_halo(c):
        @pl.when(d < nd - 1)
        def _():
            up(c).start()

        @pl.when(d > 0)
        def _():
            down(c).start()

    def spread(buf, send, recv, c, j):
        to = mate if j == 0 else tos[j - 1]
        ref = buf.at[o, :, cut(c), :]
        return remote(ref, ref, send.at[j, c], recv.at[j, c], (to, d))

    def forward(buf, send, recv, c, j):
        ref = buf.at[froms[j - 1], :, cut(c), :]
        return remote(ref, ref, send.at[j - 1, c], recv.at[j - 1, c], (mate, d))

    def start_spread(buf, send, recv, c):
        for j in list(range(1, nx)) + [0]:
            spread(buf, send, recv, c, j).start()

    def pass_on(buf, recv, send_f, recv_f, c):
        for j in range(1, nx):
            spread(buf, recv, recv, c, j).wait_recv()
            forward(buf, send_f, recv_f, c, j).start()

    start_halo(0)
    if chunks > 1:
        start_halo(1)
    for c in range(chunks):
        start_spread(orbs, c_s, c_r, c)

    @pl.when(d == 0)
    def _():
        halo[0] = jnp.zeros(halo.shape[1:], jnp.float32)

    @pl.when(d == nd - 1)
    def _():
        halo[1] = jnp.zeros(halo.shape[1:], jnp.float32)

    away = jnp.abs(
        lax.broadcasted_iota(jnp.int32, (128, 128), 0) - lax.broadcasted_iota(jnp.int32, (128, 128), 1)
    )
    band = jnp.zeros((128, 128), jnp.float32)
    for k in range(1, width + 1):
        band = jnp.where(away == k, -0.5 * coeffs[k], band)
    band = split(band)

    def stencil(c):
        at = cut(c)

        def line(p, y):
            if p < 0:
                return halo[0, (p + width) * lines + y, at, :]
            if p >= planes:
                return halo[1, (p - planes) * lines + y, at, :]
            return orbs[o, p * lines + y, at, :]

        for p in range(planes):
            mid = orbs[o, pl.ds(p * lines, lines), at, :]
            along = dot3(split(mid.reshape(lines * size, 128)), band, NN).reshape(lines, size, 128)
            for y in range(lines):
                total = along[y] + (pot[p * lines + y] - 1.5 * coeffs[0]) * line(p, y)
                for k in range(1, width + 1):
                    near_ = line(p + k, y) + line(p - k, y)
                    if y + k < lines:
                        near_ = near_ + line(p, y + k)
                    if y - k >= 0:
                        near_ = near_ + line(p, y - k)
                    total = total + (-0.5 * coeffs[k]) * near_
                images[o, p * lines + y, at, :] = total

    def step(c):
        @pl.when(d > 0)
        def _():
            up(c).wait_recv()

        @pl.when(d < nd - 1)
        def _():
            down(c).wait_recv()

        stencil(c)
        start_spread(images, i_s, i_r, c)
        pass_on(orbs, c_r, cf_s, cf_r, c)

    group = next(g for g in (4, 2, 1) if rows % g == 0)

    def gathered(buf, r):
        return jnp.concatenate(
            [jnp.concatenate([buf[s, r * group + i] for i in range(group)], axis=1) for s in range(no)], axis=0
        )

    def mine(buf, r, begin, end):
        return jnp.concatenate([buf[o, r * group + i, begin:end, :] for i in range(group)], axis=1)

    def overlaps(slot):
        height = heights[slot]
        share = height // nd
        acc[0:height, :] = jnp.zeros((height, count), jnp.float32)

        def body(r, carry):
            if slot == 1:
                left = mine(images, r, last * size, block)
            elif last == 0:
                left = mine(orbs, r, 0, block)
            else:
                left = jnp.concatenate([mine(orbs, r, 0, block), mine(images, r, 0, last * size)], axis=0)
            acc[0:height, :] += dot3(split(left), split(gathered(orbs, r)), NT)
            return carry

        lax.fori_loop(0, rows // group, body, 0)
        for e in range(nd):
            part[slot][e] = acc[e * share : (e + 1) * share, :]

    def scatter(slot, j):
        e = lax.rem(d + j, nd)
        return remote(
            part[slot].at[e], inbox[slot].at[d], rs_s.at[slot, j - 1], rs_r.at[slot, j - 1], (o, e)
        )

    def share_out(slot, j):
        e = lax.rem(d + j, nd)
        ref = full[slot].at[d]
        return remote(ref, ref, ag_s.at[slot, j - 1], ag_r.at[slot, j - 1], (o, e))

    def reduce_start(slot):
        for j in range(1, nd):
            scatter(slot, j).start()
        inbox[slot][d] = part[slot][d]

    def reduce_mid(slot):
        for j in range(1, nd):
            scatter(slot, j).wait_recv()
        total = inbox[slot][0]
        for e in range(1, nd):
            total = total + inbox[slot][e]
        full[slot][d] = total * (1.0 / cells)
        for j in range(1, nd):
            share_out(slot, j).start()

    def reduce_end(slot):
        for j in range(1, nd):
            share_out(slot, j).wait_recv()

    def early(c, carry):
        @pl.when(c + 2 < chunks)
        def _():
            start_halo(c + 2)

        step(c)

        @pl.when(c > 0)
        def _():
            pass_on(images, i_r, if_s, if_r, c - 1)

        return carry

    lax.fori_loop(0, chunks - 1, early, 0)
    pass_on(orbs, c_r, cf_s, cf_r, last)

    def arrive(c, carry):
        spread(orbs, c_s, c_r, c, 0).wait_recv()
        for j in range(1, nx):
            forward(orbs, cf_s, cf_r, c, j).wait_recv()
        return carry

    lax.fori_loop(0, chunks, arrive, 0)
    overlaps(0)
    reduce_start(0)

    @pl.when(d > 0)
    def _():
        up(last).wait_recv()

    @pl.when(d < nd - 1)
    def _():
        down(last).wait_recv()

    stencil(last)
    start_spread(images, i_s, i_r, last)
    overlaps(1)
    reduce_start(1)
    reduce_mid(0)
    reduce_mid(1)
    if chunks > 1:
        pass_on(images, i_r, if_s, if_r, last - 1)
    pass_on(images, i_r, if_s, if_r, last)
    reduce_end(0)

    def arrive_images(c, carry):
        spread(images, i_s, i_r, c, 0).wait_recv()
        for j in range(1, nx):
            forward(images, if_s, if_r, c, j).wait_recv()
        return carry

    lax.fori_loop(0, chunks, arrive_images, 0)
    reduce_end(1)
    pltpu.make_async_copy(pg, pg, local_sem.at[1]).wait()

    def matrix(slot):
        return jnp.concatenate([full[slot][e] for e in range(nd)], axis=0)

    def fold(value):
        return jnp.sum(value.reshape(block // 8, 8, 128), axis=0)

    first = matrix(0)
    correlation = split(first[:block])
    hamilton = split(jnp.concatenate([first[block:], matrix(1)], axis=0) if last else matrix(1))

    def gradient(r, sums):
        mixed = dot3(correlation, split(gathered(images, r)), NN) + dot3(hamilton, split(gathered(orbs, r)), NN)
        both, cross, before = sums
        for i in range(group):
            at = r * group + i
            grad = 4.0 * images[o, at] - 2.0 * mixed[:, i * 128 : (i + 1) * 128]
            grad_out[at] = grad
            old = pg[at]
            both = both + fold(grad * grad)
            cross = cross + fold(grad * old)
            before = before + fold(old * old)
        return both, cross, before

    zero = jnp.zeros((8, 128), jnp.float32)
    sums = lax.fori_loop(0, rows // group, gradient, (zero, zero, zero))

    near[o] = jnp.concatenate(
        [jnp.sum(s, axis=0, keepdims=True) for s in sums] + [jnp.zeros((5, 128), jnp.float32)], axis=0
    )

    def tell(buf, at, j, send, recv, device):
        return remote(buf.at[at], buf.at[at], send.at[j - 1], recv.at[j - 1], device)

    def near_copy(j):
        return tell(near, o, j, n_s, n_r, (lax.rem(o + j, no), d))

    def far_copy(j):
        return tell(far, d, j, f_s, f_r, (o, lax.rem(d + j, nd)))

    for j in range(1, no):
        near_copy(j).start()
    for j in range(1, no):
        near_copy(j).wait_recv()
    total = near[0]
    for s in range(1, no):
        total = total + near[s]
    far[d] = total
    for j in range(1, nd):
        far_copy(j).start()
    for j in range(1, nd):
        far_copy(j).wait_recv()
    total = far[0]
    for s in range(1, nd):
        total = total + far[s]
    stat_out[...] = total

    def drain(c, carry):
        @pl.when(d < nd - 1)
        def _():
            up(c).wait_send()

        @pl.when(d > 0)
        def _():
            down(c).wait_send()

        for j in range(nx):
            spread(orbs, c_s, c_r, c, j).wait_send()
            spread(images, i_s, i_r, c, j).wait_send()
        for j in range(1, nx):
            forward(orbs, cf_s, cf_r, c, j).wait_send()
            forward(images, if_s, if_r, c, j).wait_send()
        return carry

    lax.fori_loop(0, chunks, drain, 0)
    for j in range(1, nd):
        for slot in range(2):
            scatter(slot, j).wait_send()
            share_out(slot, j).wait_send()
        far_copy(j).wait_send()
    for j in range(1, no):
        near_copy(j).wait_send()


def on_device(no, nd, orbitals, potential, prev_gradient, prev_direction):
    block, planes, lines, columns = orbitals.shape
    rows = planes * lines
    chunks = next(n for n in (3, 2, 1) if block % (8 * n) == 0)
    nx = no // 2
    late = block // chunks
    early = 2 * block - late
    f32 = jnp.float32
    dma = pltpu.SemaphoreType.DMA
    turned = orbitals.reshape(block, rows, columns).transpose(1, 0, 2)
    links = max(nx - 1, 1)
    grad, stats = pl.pallas_call(
        functools.partial(kernel, (no, nd, planes, lines, block, chunks)),
        out_shape=(
            jax.ShapeDtypeStruct((rows, block, columns), f32),
            jax.ShapeDtypeStruct((8, columns), f32),
        ),
        in_specs=[
            pl.BlockSpec(memory_space=pl.ANY),
            pl.BlockSpec(memory_space=pltpu.VMEM),
            pl.BlockSpec(memory_space=pl.ANY),
        ],
        out_specs=(pl.BlockSpec(memory_space=pltpu.VMEM), pl.BlockSpec(memory_space=pltpu.VMEM)),
        scratch_shapes=[
            pltpu.VMEM((no, rows, block, columns), f32),
            pltpu.VMEM((no, rows, block, columns), f32),
            pltpu.VMEM((2, width * lines, block, columns), f32),
            pltpu.VMEM((rows, block, columns), f32),
            *[pltpu.VMEM((nd, early // nd, no * block), f32)] * 3,
            *[pltpu.VMEM((nd, late // nd, no * block), f32)] * 3,
            pltpu.VMEM((early, no * block), f32),
            pltpu.VMEM((no, 8, columns), f32),
            pltpu.VMEM((nd, 8, columns), f32),
            dma((2,)),
            dma((2, chunks)), dma((2, chunks)),
            dma((nx, chunks)), dma((nx, chunks)), dma((links, chunks)), dma((links, chunks)),
            dma((nx, chunks)), dma((nx, chunks)), dma((links, chunks)), dma((links, chunks)),
            dma((2, nd - 1)), dma((2, nd - 1)), dma((2, nd - 1)), dma((2, nd - 1)),
            dma((no - 1,)), dma((no - 1,)), dma((nd - 1,)), dma((nd - 1,)),
        ],
        compiler_params=pltpu.CompilerParams(
            collective_id=0, has_side_effects=True, vmem_limit_bytes=60 * 1024 * 1024
        ),
    )(turned, potential.reshape(rows, 1, columns), prev_gradient)
    grad = grad.transpose(1, 0, 2).reshape(orbitals.shape)
    both, cross, before = jnp.sum(stats[0]), jnp.sum(stats[1]), jnp.sum(stats[2])
    beta = (both - cross) / before
    direction = -grad + beta * prev_direction
    return (orbitals + step_length * direction, direction, grad)


def solution(mesh):
    spec = P("orb", "dom", None, None)
    return jax.shard_map(
        functools.partial(on_device, mesh.shape["orb"], mesh.shape["dom"]),
        mesh=mesh,
        in_specs=(spec, P("dom", None, None), spec, spec),
        out_specs=(spec, spec, spec),
        check_vma=False,
    )
```

```python
import functools

import jax
import jax.numpy as jnp
from jax import lax
from jax.experimental import pallas as pl
from jax.experimental.pallas import tpu as pltpu
from jax.sharding import PartitionSpec as P

coeffs = (-205.0 / 72.0, 8.0 / 5.0, -1.0 / 5.0, 8.0 / 315.0, -1.0 / 560.0)
step_length = 0.05
width = 4
MESH = pl.DeviceIdType.MESH
NT = (((1,), (1,)), ((), ()))
NN = (((1,), (0,)), ((), ()))


def split(value):
    high = value.astype(jnp.bfloat16)
    return high, (value - high.astype(jnp.float32)).astype(jnp.bfloat16)


def dot3(left, right, dims):
    def dot(a, b):
        return lax.dot_general(a, b, dims, preferred_element_type=jnp.float32)

    return dot(left[0], right[0]) + (dot(left[0], right[1]) + dot(left[1], right[0]))


def kernel(
    cfg, c_hbm, pot, pg_hbm, grad_out, stat_out,
    orbs, images, halo, pg, part0, inbox0, full0, part1, inbox1, full1, acc, near, far,
    local_sem, halo_s, halo_r, c_s, c_r, cf_s, cf_r, i_s, i_r, if_s, if_r,
    rs_s, rs_r, ag_s, ag_r, n_s, n_r, f_s, f_r,
):
    no, nd, planes, lines, block, chunks = cfg
    rows = planes * lines
    edge = width * lines
    size = block // chunks
    nx = no // 2
    count = no * block
    cells = rows * 128 * nd
    last = chunks - 1
    heights = (block + last * size, size)
    part, inbox, full = (part0, part1), (inbox0, inbox1), (full0, full1)
    o, d = lax.axis_index("orb"), lax.axis_index("dom")
    core = lax.rem(o, 2)
    column = o // 2
    mate = column * 2 + (1 - core)
    tos = [lax.rem(column + j, nx) * 2 + core for j in range(1, nx)]
    froms = [lax.rem(column - j + nx, nx) * 2 + core for j in range(1, nx)]

    load = pltpu.make_async_copy(c_hbm, orbs.at[o], local_sem.at[0])
    load.start()
    for r in range(rows):
        pltpu.make_async_copy(
            pg_hbm.at[:, r // lines, r % lines, :], pg.at[r], local_sem.at[1]
        ).start()

    barrier = pltpu.get_barrier_semaphore()
    for j in range(1, no):
        pl.semaphore_signal(barrier, inc=1, device_id=(lax.rem(o + j, no), d), device_id_type=MESH)
    for j in range(1, nd):
        pl.semaphore_signal(barrier, inc=1, device_id=(o, lax.rem(d + j, nd)), device_id_type=MESH)
    load.wait()
    pl.semaphore_wait(barrier, no + nd - 2)

    def cut(c):
        return pl.ds(pl.multiple_of(c * size, 8), size)

    def remote(src, dst, send, recv, device):
        return pltpu.make_async_remote_copy(
            src_ref=src, dst_ref=dst, send_sem=send, recv_sem=recv, device_id=device, device_id_type=MESH
        )

    def up(c):
        return remote(
            orbs.at[o, pl.ds(rows - edge, edge), cut(c), :], halo.at[0, :, cut(c), :],
            halo_s.at[0, c], halo_r.at[0, c], (o, lax.rem(d + 1, nd)),
        )

    def down(c):
        return remote(
            orbs.at[o, pl.ds(0, edge), cut(c), :], halo.at[1, :, cut(c), :],
            halo_s.at[1, c], halo_r.at[1, c], (o, lax.rem(d + nd - 1, nd)),
        )

    def start_halo(c):
        @pl.when(d < nd - 1)
        def _():
            up(c).start()

        @pl.when(d > 0)
        def _():
            down(c).start()

    def spread(buf, send, recv, c, j):
        to = mate if j == 0 else tos[j - 1]
        ref = buf.at[o, :, cut(c), :]
        return remote(ref, ref, send.at[j, c], recv.at[j, c], (to, d))

    def forward(buf, send, recv, c, j):
        ref = buf.at[froms[j - 1], :, cut(c), :]
        return remote(ref, ref, send.at[j - 1, c], recv.at[j - 1, c], (mate, d))

    def start_spread(buf, send, recv, c):
        for j in list(range(1, nx)) + [0]:
            spread(buf, send, recv, c, j).start()

    def pass_on(buf, recv, send_f, recv_f, c):
        for j in range(1, nx):
            spread(buf, recv, recv, c, j).wait_recv()
            forward(buf, send_f, recv_f, c, j).start()

    start_halo(0)
    for c in range(chunks):
        start_spread(orbs, c_s, c_r, c)

    @pl.when(d == 0)
    def _():
        halo[0] = jnp.zeros(halo.shape[1:], jnp.float32)

    @pl.when(d == nd - 1)
    def _():
        halo[1] = jnp.zeros(halo.shape[1:], jnp.float32)

    away = jnp.abs(
        lax.broadcasted_iota(jnp.int32, (128, 128), 0) - lax.broadcasted_iota(jnp.int32, (128, 128), 1)
    )
    band = jnp.zeros((128, 128), jnp.float32)
    for k in range(1, width + 1):
        band = jnp.where(away == k, -0.5 * coeffs[k], band)
    band = split(band)

    def stencil(c):
        at = cut(c)

        def line(p, y):
            if p < 0:
                return halo[0, (p + width) * lines + y, at, :]
            if p >= planes:
                return halo[1, (p - planes) * lines + y, at, :]
            return orbs[o, p * lines + y, at, :]

        for p in range(planes):
            mid = orbs[o, pl.ds(p * lines, lines), at, :]
            along = dot3(split(mid.reshape(lines * size, 128)), band, NN).reshape(lines, size, 128)
            for y in range(lines):
                total = along[y] + (pot[p * lines + y] - 1.5 * coeffs[0]) * line(p, y)
                for k in range(1, width + 1):
                    near_ = line(p + k, y) + line(p - k, y)
                    if y + k < lines:
                        near_ = near_ + line(p, y + k)
                    if y - k >= 0:
                        near_ = near_ + line(p, y - k)
                    total = total + (-0.5 * coeffs[k]) * near_
                images[o, p * lines + y, at, :] = total

    def step(c):
        @pl.when(d > 0)
        def _():
            up(c).wait_recv()

        @pl.when(d < nd - 1)
        def _():
            down(c).wait_recv()

        start_halo(c + 1)
        stencil(c)
        start_spread(images, i_s, i_r, c)
        pass_on(orbs, c_r, cf_s, cf_r, c)

    group = next(g for g in (4, 2, 1) if rows % g == 0)

    def gathered(buf, r):
        return jnp.concatenate(
            [jnp.concatenate([buf[s, r * group + i] for i in range(group)], axis=1) for s in range(no)], axis=0
        )

    def mine(buf, r, begin, end):
        return jnp.concatenate([buf[o, r * group + i, begin:end, :] for i in range(group)], axis=1)

    def overlaps(slot):
        height = heights[slot]
        share = height // nd
        acc[0:height, :] = jnp.zeros((height, count), jnp.float32)

        def body(r, carry):
            if slot == 1:
                left = mine(images, r, last * size, block)
            elif last == 0:
                left = mine(orbs, r, 0, block)
            else:
                left = jnp.concatenate([mine(orbs, r, 0, block), mine(images, r, 0, last * size)], axis=0)
            acc[0:height, :] += dot3(split(left), split(gathered(orbs, r)), NT)
            return carry

        lax.fori_loop(0, rows // group, body, 0)
        for e in range(nd):
            part[slot][e] = acc[e * share : (e + 1) * share, :]

    def scatter(slot, j):
        e = lax.rem(d + j, nd)
        return remote(
            part[slot].at[e], inbox[slot].at[d], rs_s.at[slot, j - 1], rs_r.at[slot, j - 1], (o, e)
        )

    def share_out(slot, j):
        e = lax.rem(d + j, nd)
        ref = full[slot].at[d]
        return remote(ref, ref, ag_s.at[slot, j - 1], ag_r.at[slot, j - 1], (o, e))

    def reduce_start(slot):
        for j in range(1, nd):
            scatter(slot, j).start()
        inbox[slot][d] = part[slot][d]

    def reduce_mid(slot):
        for j in range(1, nd):
            scatter(slot, j).wait_recv()
        total = inbox[slot][0]
        for e in range(1, nd):
            total = total + inbox[slot][e]
        full[slot][d] = total * (1.0 / cells)
        for j in range(1, nd):
            share_out(slot, j).start()

    def reduce_end(slot):
        for j in range(1, nd):
            share_out(slot, j).wait_recv()

    def early(c, carry):
        step(c)

        @pl.when(c > 0)
        def _():
            pass_on(images, i_r, if_s, if_r, c - 1)

        return carry

    lax.fori_loop(0, chunks - 1, early, 0)
    pass_on(orbs, c_r, cf_s, cf_r, last)

    def arrive(c, carry):
        spread(orbs, c_s, c_r, c, 0).wait_recv()
        for j in range(1, nx):
            forward(orbs, cf_s, cf_r, c, j).wait_recv()
        return carry

    lax.fori_loop(0, chunks, arrive, 0)
    overlaps(0)
    reduce_start(0)

    @pl.when(d > 0)
    def _():
        up(last).wait_recv()

    @pl.when(d < nd - 1)
    def _():
        down(last).wait_recv()

    stencil(last)
    start_spread(images, i_s, i_r, last)
    overlaps(1)
    reduce_start(1)
    reduce_mid(0)
    reduce_mid(1)
    if chunks > 1:
        pass_on(images, i_r, if_s, if_r, last - 1)
    pass_on(images, i_r, if_s, if_r, last)
    reduce_end(0)

    def arrive_images(c, carry):
        spread(images, i_s, i_r, c, 0).wait_recv()
        for j in range(1, nx):
            forward(images, if_s, if_r, c, j).wait_recv()
        return carry

    lax.fori_loop(0, chunks, arrive_images, 0)
    reduce_end(1)
    pltpu.make_async_copy(pg, pg, local_sem.at[1]).wait()

    def matrix(slot):
        return jnp.concatenate([full[slot][e] for e in range(nd)], axis=0)

    def fold(value):
        return jnp.sum(value.reshape(block // 8, 8, 128), axis=0)

    first = matrix(0)
    correlation = split(first[:block])
    hamilton = split(jnp.concatenate([first[block:], matrix(1)], axis=0) if last else matrix(1))

    def gradient(r, sums):
        mixed = dot3(correlation, split(gathered(images, r)), NN) + dot3(hamilton, split(gathered(orbs, r)), NN)
        both, cross, before = sums
        for i in range(group):
            at = r * group + i
            grad = 4.0 * images[o, at] - 2.0 * mixed[:, i * 128 : (i + 1) * 128]
            grad_out[at] = grad
            old = pg[at]
            both = both + fold(grad * grad)
            cross = cross + fold(grad * old)
            before = before + fold(old * old)
        return both, cross, before

    zero = jnp.zeros((8, 128), jnp.float32)
    sums = lax.fori_loop(0, rows // group, gradient, (zero, zero, zero))

    near[o] = jnp.concatenate(
        [jnp.sum(s, axis=0, keepdims=True) for s in sums] + [jnp.zeros((5, 128), jnp.float32)], axis=0
    )

    def tell(buf, at, j, send, recv, device):
        return remote(buf.at[at], buf.at[at], send.at[j - 1], recv.at[j - 1], device)

    def near_copy(j):
        return tell(near, o, j, n_s, n_r, (lax.rem(o + j, no), d))

    def far_copy(j):
        return tell(far, d, j, f_s, f_r, (o, lax.rem(d + j, nd)))

    for j in range(1, no):
        near_copy(j).start()
    for j in range(1, no):
        near_copy(j).wait_recv()
    total = near[0]
    for s in range(1, no):
        total = total + near[s]
    far[d] = total
    for j in range(1, nd):
        far_copy(j).start()
    for j in range(1, nd):
        far_copy(j).wait_recv()
    total = far[0]
    for s in range(1, nd):
        total = total + far[s]
    stat_out[...] = total

    def drain(c, carry):
        @pl.when(d < nd - 1)
        def _():
            up(c).wait_send()

        @pl.when(d > 0)
        def _():
            down(c).wait_send()

        for j in range(nx):
            spread(orbs, c_s, c_r, c, j).wait_send()
            spread(images, i_s, i_r, c, j).wait_send()
        for j in range(1, nx):
            forward(orbs, cf_s, cf_r, c, j).wait_send()
            forward(images, if_s, if_r, c, j).wait_send()
        return carry

    lax.fori_loop(0, chunks, drain, 0)
    for j in range(1, nd):
        for slot in range(2):
            scatter(slot, j).wait_send()
            share_out(slot, j).wait_send()
        far_copy(j).wait_send()
    for j in range(1, no):
        near_copy(j).wait_send()


def on_device(no, nd, orbitals, potential, prev_gradient, prev_direction):
    block, planes, lines, columns = orbitals.shape
    rows = planes * lines
    chunks = next(n for n in (3, 2, 1) if block % (8 * n) == 0)
    nx = no // 2
    late = block // chunks
    early = 2 * block - late
    f32 = jnp.float32
    dma = pltpu.SemaphoreType.DMA
    turned = orbitals.reshape(block, rows, columns).transpose(1, 0, 2)
    links = max(nx - 1, 1)
    grad, stats = pl.pallas_call(
        functools.partial(kernel, (no, nd, planes, lines, block, chunks)),
        out_shape=(
            jax.ShapeDtypeStruct((rows, block, columns), f32),
            jax.ShapeDtypeStruct((8, columns), f32),
        ),
        in_specs=[
            pl.BlockSpec(memory_space=pl.ANY),
            pl.BlockSpec(memory_space=pltpu.VMEM),
            pl.BlockSpec(memory_space=pl.ANY),
        ],
        out_specs=(pl.BlockSpec(memory_space=pltpu.VMEM), pl.BlockSpec(memory_space=pltpu.VMEM)),
        scratch_shapes=[
            pltpu.VMEM((no, rows, block, columns), f32),
            pltpu.VMEM((no, rows, block, columns), f32),
            pltpu.VMEM((2, width * lines, block, columns), f32),
            pltpu.VMEM((rows, block, columns), f32),
            *[pltpu.VMEM((nd, early // nd, no * block), f32)] * 3,
            *[pltpu.VMEM((nd, late // nd, no * block), f32)] * 3,
            pltpu.VMEM((early, no * block), f32),
            pltpu.VMEM((no, 8, columns), f32),
            pltpu.VMEM((nd, 8, columns), f32),
            dma((2,)),
            dma((2, chunks)), dma((2, chunks)),
            dma((nx, chunks)), dma((nx, chunks)), dma((links, chunks)), dma((links, chunks)),
            dma((nx, chunks)), dma((nx, chunks)), dma((links, chunks)), dma((links, chunks)),
            dma((2, nd - 1)), dma((2, nd - 1)), dma((2, nd - 1)), dma((2, nd - 1)),
            dma((no - 1,)), dma((no - 1,)), dma((nd - 1,)), dma((nd - 1,)),
        ],
        compiler_params=pltpu.CompilerParams(
            collective_id=0, has_side_effects=True, vmem_limit_bytes=60 * 1024 * 1024
        ),
    )(turned, potential.reshape(rows, 1, columns), prev_gradient)
    grad = grad.transpose(1, 0, 2).reshape(orbitals.shape)
    both, cross, before = jnp.sum(stats[0]), jnp.sum(stats[1]), jnp.sum(stats[2])
    beta = (both - cross) / before
    direction = -grad + beta * prev_direction
    return (orbitals + step_length * direction, direction, grad)


def solution(mesh):
    spec = P("orb", "dom", None, None)
    return jax.shard_map(
        functools.partial(on_device, mesh.shape["orb"], mesh.shape["dom"]),
        mesh=mesh,
        in_specs=(spec, P("dom", None, None), spec, spec),
        out_specs=(spec, spec, spec),
        check_vma=False,
    )
```
